256 devices in a mesh: grp: 8 (over y, core), box: 32 (over z, x).
Axes of the slice: x: 4, y: 4, z: 8, core: 2. Of those that a mesh axis runs over, the one named last changes fastest.
Arguments:
- leaves: bfloat16 [2048, 64, 1024], P(('grp', 'box')), may hold values from -6 to 6
- translate: bfloat16 [12, 2048, 64, 256], P(None, ('grp', 'box')), may hold values from -0.375 to 0.375
- local_links: int32 [12, 2, 2048], P(None, None, ('grp', 'box')), may hold values from 0 to 7
- remote_links: int32 [12, 2, 2048], P(None, None, ('grp', 'box')), may hold values from 0 to 3
Outputs:
- coefficients: bfloat16 [2048, 64, 1024], P(('grp', 'box'))
The draws below stay inside these ranges and needn't reach their ends.
Inputs may be any that keep to these rules, and one draw needn't show every extreme that they name: `local_links`: places among a device's own 8 nodes. `remote_links`: places among the partner's leading 4 nodes.
All inputs are finite; a program needn't handle non-finite values.
Results may differ from the reference program's by a relative error of at most 0.025.
Values may be sent and summed in bfloat16 or wider, within the bound.
A program may use at most 64 MiB of HBM per device.

```python
import jax
import jax.numpy as jnp
from jax import lax

R = 64
TRACES = 1024
NODES = 8
SEND = 4
LEVELS = 12
ALL_NODES = 2048
N_GRP = 8
N_BOX = 32


def set_ends(drawn, stream_key, smallest, top_value):
    index_at = [jax.random.randint(jax.random.fold_in(stream_key, axis), (), 0, length) for axis, length in enumerate(drawn.shape)]
    longest = drawn.shape.index(max(drawn.shape))
    next_to = index_at[:longest] + [(index_at[longest] + 1) % drawn.shape[longest]] + index_at[longest + 1:]
    return drawn.at[tuple(index_at)].set(smallest).at[tuple(next_to)].set(top_value)


def block_scale(key, dims, cuts, smallest, largest):
    factor_of, own = 1.0, jax.random.fold_in(key, 6)
    for dim, blocks in cuts:
        draws = jnp.exp(jax.random.uniform(jax.random.fold_in(own, dim), (blocks,), jnp.float32, smallest / len(cuts), largest / len(cuts)))
        factor_of = factor_of * jnp.repeat(draws, dims[dim] // blocks).reshape([-1 if axis == dim else 1 for axis in range(len(dims))])
    return factor_of


def gaussian(rng, shape, deviation, most, cuts=(), kind=jnp.bfloat16):
    array = deviation * jax.random.normal(rng, shape, jnp.float32)
    if cuts:
        array = array * block_scale(rng, shape, cuts, -0.22, 0.18)
    return jnp.clip(array, -most, most).astype(kind)


def setup_inputs(seed: int = 0) -> dict:
    arg_keys = jax.random.split(jax.random.key(seed), 5)
    leaves = gaussian(arg_keys[0], (ALL_NODES, R, TRACES), 1.0, 6.0, ((0, 256),))
    translate = gaussian(arg_keys[1], (LEVELS, ALL_NODES, R, 4 * R), (4 * R) ** -0.5, 0.375, ((1, 256),))
    local_links = set_ends(jax.random.randint(arg_keys[2], (LEVELS, 2, ALL_NODES), 0, NODES), jax.random.fold_in(arg_keys[2], 1), 0, NODES - 1).astype(jnp.int32)
    remote_links = set_ends(jax.random.randint(arg_keys[3], (LEVELS, 2, ALL_NODES), 0, SEND), jax.random.fold_in(arg_keys[3], 1), 0, SEND - 1).astype(jnp.int32)
    return {"leaves": leaves, "translate": translate, "local_links": local_links, "remote_links": remote_links}


def advance(current, blocks_level, near_links, far_links, swap_bit):
    devices = N_GRP * N_BOX
    partner_order = jnp.bitwise_xor(jnp.arange(N_BOX), 1 << swap_bit)
    partner_rows = current[:, partner_order, :SEND].reshape(devices, SEND, R, TRACES)
    flat_rows = current.reshape(devices, NODES, R, TRACES)
    matrices = blocks_level.reshape(devices, NODES, R, 4 * R)
    near_dev = near_links.reshape(2, devices, NODES).transpose(1, 0, 2)
    far_dev = far_links.reshape(2, devices, NODES).transpose(1, 0, 2)

    def one_device(pieces):
        own_rows, other_rows, matrix, near_idx, far_idx = pieces
        stacked = jnp.concatenate([own_rows[near_idx[0]], own_rows[near_idx[1]], other_rows[far_idx[0]], other_rows[far_idx[1]]], axis=1)
        summed = jnp.einsum("nrk,nkb->nrb", matrix.astype(jnp.float32), stacked.astype(jnp.float32))
        return summed.astype(jnp.bfloat16)

    result = lax.map(one_device, (flat_rows, partner_rows, matrices, near_dev, far_dev))
    return result.reshape(N_GRP, N_BOX, NODES, R, TRACES)


def switch_groups(current):
    block_rows = NODES // N_GRP
    split_rows = current.reshape(N_GRP, N_BOX, N_GRP, block_rows, R, TRACES)
    return split_rows.transpose(2, 1, 0, 3, 4, 5).reshape(N_GRP, N_BOX, NODES, R, TRACES)


def reference(leaves, translate, local_links, remote_links):
    current = leaves.reshape(N_GRP, N_BOX, NODES, R, TRACES)
    box_bits = int(N_BOX).bit_length() - 1
    half_levels = LEVELS // 2
    for layer_index in range(LEVELS):
        if layer_index == half_levels:
            current = switch_groups(current)
        swap_bit = (layer_index % half_levels) % box_bits
        current = advance(current, translate[layer_index], local_links[layer_index], remote_links[layer_index], swap_bit)
    return current.reshape(N_GRP * N_BOX * NODES, R, TRACES)
```

```python
import functools

import jax
import jax.numpy as jnp
from jax import lax
from jax.experimental import pallas as pl
from jax.experimental.pallas import tpu as pltpu
from jax.sharding import PartitionSpec as P

MESH = pl.DeviceIdType.MESH
SEND = 4
CHUNKS = 4
STEP_AT = (0.0, 4.0, 8.0, 12.0, 17.0, 23.0, 27.0, 31.0, 35.0, 39.0, 43.0, 48.0, 54.0)
STAGGER = 9.0
AHEAD = 2


def flipped(index, mask):
    return index + mask - 2 * mask * lax.rem(index // mask, 2)


def kernel(
    sizes, leaves, translate, near, far, out, z, w, tv, send, recv, sw_send, sw_recv, leaf_sem, tr_sem, out_sem
):
    levels, nodes, rank, cols, groups, box_bits = sizes
    half = levels // 2
    pre, last = levels, levels + 1
    q = lax.axis_index("grp")
    b = lax.axis_index("box")
    lead = SEND * rank
    depth = nodes * rank

    def partner(level):
        return (q, flipped(b, 1 << (level % half % box_bits)))

    def columns(s):
        return pl.ds(s * cols, cols)

    def out_place(level):
        return pre if level == half - 1 else last if level == levels - 1 else level + 1

    def exchange(level, s):
        if level == 0:
            src = leaves.at[pl.ds(0, SEND), :, columns(s)]
        else:
            src = z.at[level, s, pl.ds(0, SEND)]
        return pltpu.make_async_remote_copy(
            src,
            z.at[level, s, pl.ds(nodes, SEND)],
            send.at[level, s],
            recv.at[level, s],
            device_id=partner(level),
            device_id_type=MESH,
        )

    def switch(s, r):
        to = lax.rem(q + r, groups)
        return pltpu.make_async_remote_copy(
            z.at[pre, s, to],
            z.at[half, s, q],
            sw_send.at[s, r - 1],
            sw_recv.at[s, r - 1],
            device_id=(to, b),
            device_id_type=MESH,
        )

    def leaf_copy(s):
        return pltpu.make_async_copy(
            leaves.at[:, :, columns(s)], z.at[0, s, pl.ds(0, nodes)], leaf_sem.at[s]
        )

    def tr_copy(level):
        return pltpu.make_async_copy(translate.at[level], tv.at[level], tr_sem.at[level])

    def out_copy(s):
        return pltpu.make_async_copy(
            z.at[last, s, pl.ds(0, nodes)], out.at[:, :, columns(s)], out_sem.at[s]
        )

    lane = lax.broadcasted_iota(jnp.int32, (rank, 2 * rank), 1)
    left = lane < rank
    side = jnp.where(left, 0, 1)

    def build(level):
        tr_copy(level).wait()

        def one(n, carry):
            rows = pl.ds(pl.multiple_of(n * rank, rank), rank)
            for links, count, first in ((near, nodes, 0), (far, SEND, nodes)):
                pair = tv[level, n, :, pl.ds(0 if first == 0 else 2 * rank, 2 * rank)].astype(jnp.float32)
                turned = pltpu.roll(pair, rank, 1)
                one_link = links[level, 0, n]
                two_link = links[level, 1, n]
                at_pair = jnp.where(left, one_link, two_link) - side
                at_turned = jnp.where(left, two_link, one_link) - side
                for j in range(count // 2):
                    spread = jnp.where(at_pair == 2 * j, pair, 0.0) + jnp.where(at_turned == 2 * j, turned, 0.0)
                    w[level, rows, pl.ds((first + 2 * j) * rank, 2 * rank)] = spread.astype(w.dtype)
            return carry

        lax.fori_loop(0, nodes, one, 0)

    def product(level, s, first):
        stacked = z[level, s].reshape((nodes + SEND) * rank, cols)
        summed = jnp.dot(w[level, pl.ds(first * rank, lead), :], stacked, preferred_element_type=jnp.float32)
        z[out_place(level), s, pl.ds(first, SEND)] = summed.astype(z.dtype).reshape(SEND, rank, cols)

    def step(level, s):
        if level == 0:
            leaf_copy(s).wait()
        exchange(level, s).wait_recv()
        product(level, s, 0)
        if level + 1 < levels and level + 1 != half:
            exchange(level + 1, s).start()
        product(level, s, SEND)
        if level + 1 == half:
            for r in range(1, groups):
                switch(s, r).start()
            z[half, s, q] = z[pre, s, q]
        if level + 1 == levels:
            out_copy(s).start()

    def forward(s):
        for r in range(1, groups):
            switch(s, r).wait_recv()
        exchange(half, s).start()

    barrier = pltpu.get_barrier_semaphore()
    for bit in range(box_bits):
        pl.semaphore_signal(barrier, inc=1, device_id=partner(bit), device_id_type=MESH)
    for r in range(1, groups):
        pl.semaphore_signal(barrier, inc=1, device_id=(lax.rem(q + r, groups), b), device_id_type=MESH)
    for s in range(CHUNKS):
        leaf_copy(s).start()
        if s == 0:
            tr_copy(0).start()
    for level in range(1, levels):
        tr_copy(level).start()
    pl.semaphore_wait(barrier, box_bits + groups - 1)
    for s in range(min(AHEAD, CHUNKS)):
        exchange(0, s).start()
    build(0)

    tasks = sorted((STEP_AT[i] + STAGGER * s, i, s) for s in range(CHUNKS) for i in range(levels + 1))
    for _, i, s in tasks:
        if i == half:
            forward(s)
            continue
        level = i if i < half else i - 1
        step(level, s)
        if level == 0 and s + AHEAD < CHUNKS:
            exchange(0, s + AHEAD).start()
        if s == 0 and level + 1 < levels:
            build(level + 1)

    for s in range(CHUNKS):
        for level in range(levels):
            exchange(level, s).wait_send()
        for r in range(1, groups):
            switch(s, r).wait_send()
        out_copy(s).wait()


def on_device(leaves, translate, local_links, remote_links):
    nodes, rank, traces = leaves.shape
    levels = translate.shape[0]
    groups = lax.axis_size("grp")
    box_bits = lax.axis_size("box").bit_length() - 1
    cols = traces // CHUNKS
    width = nodes + SEND
    sizes = (levels, nodes, rank, cols, groups, box_bits)
    anywhere = pl.BlockSpec(memory_space=pl.ANY)
    scalars = pl.BlockSpec(memory_space=pltpu.SMEM)
    dma = pltpu.SemaphoreType.DMA
    return pl.pallas_call(
        functools.partial(kernel, sizes),
        out_shape=jax.ShapeDtypeStruct(leaves.shape, leaves.dtype),
        in_specs=[anywhere, anywhere, scalars, scalars],
        out_specs=anywhere,
        scratch_shapes=[
            pltpu.VMEM((levels + 2, CHUNKS, width, rank, cols), leaves.dtype),
            pltpu.VMEM((levels, nodes * rank, width * rank), leaves.dtype),
            pltpu.VMEM(translate.shape, translate.dtype),
            dma((levels, CHUNKS)),
            dma((levels, CHUNKS)),
            dma((CHUNKS, groups - 1)),
            dma((CHUNKS, groups - 1)),
            dma((CHUNKS,)),
            dma((levels,)),
            dma((CHUNKS,)),
        ],
        name="butterfly",
        compiler_params=pltpu.CompilerParams(
            collective_id=0, has_side_effects=True, vmem_limit_bytes=48 << 20
        ),
    )(leaves, translate, local_links, remote_links)


def solution(mesh):
    placed = (
        P(("grp", "box"), None, None),
        P(None, ("grp", "box"), None, None),
        P(None, None, ("grp", "box")),
        P(None, None, ("grp", "box")),
    )
    return jax.shard_map(
        on_device,
        mesh=mesh,
        in_specs=placed,
        out_specs=P(("grp", "box"), None, None),
        check_vma=False,
    )
```

```python
import functools

import jax
import jax.numpy as jnp
from jax import lax
from jax.experimental import pallas as pl
from jax.experimental.pallas import tpu as pltpu
from jax.sharding import PartitionSpec as P

MESH = pl.DeviceIdType.MESH
SEND = 4
CHUNKS = 8
BUILD = 8
ORDER = 0xf4808544008744185500744170365205844757513828320014477152354460012170640742325815464177360350257271140564063851717304045587712686251307307421243371576630032621515673327661331025656223314461576722303662581127036631225466326


def flipped(index, mask):
    return index + mask - 2 * mask * lax.rem(index // mask, 2)


def kernel(
    sizes, leaves, translate, near_in, far_in, out, z, w, tv, near, far, link_sem, send, recv, sw_send, sw_recv, leaf_sem, tr_sem, out_sem
):
    levels, nodes, rank, cols, groups, box_bits = sizes
    half = levels // 2
    pre, last = levels, levels + 1
    q = lax.axis_index("grp")
    b = lax.axis_index("box")
    lead = SEND * rank
    depth = nodes * rank

    def partner(level):
        return (q, flipped(b, 1 << (level % half % box_bits)))

    def columns(s):
        return pl.ds(s * cols, cols)

    def out_place(level):
        return pre if level == half - 1 else last if level == levels - 1 else level + 1

    def exchange(level, s):
        if level == 0:
            src = leaves.at[pl.ds(0, SEND), :, columns(s)]
        else:
            src = z.at[level, s, pl.ds(0, SEND)]
        return pltpu.make_async_remote_copy(
            src,
            z.at[level, s, pl.ds(nodes, SEND)],
            send.at[level, s],
            recv.at[level, s],
            device_id=partner(level),
            device_id_type=MESH,
        )

    def switch(s, r):
        to = lax.rem(q + r, groups)
        return pltpu.make_async_remote_copy(
            z.at[pre, s, to],
            z.at[half, s, q],
            sw_send.at[s, r - 1],
            sw_recv.at[s, r - 1],
            device_id=(to, b),
            device_id_type=MESH,
        )

    def leaf_copy(s):
        return pltpu.make_async_copy(
            leaves.at[:, :, columns(s)], z.at[0, s, pl.ds(0, nodes)], leaf_sem.at[s]
        )

    def tr_copy(level):
        return pltpu.make_async_copy(translate.at[level], tv.at[level], tr_sem.at[level])

    def out_copy(s):
        return pltpu.make_async_copy(
            z.at[last, s, pl.ds(0, nodes)], out.at[:, :, columns(s)], out_sem.at[s]
        )

    def link_copies():
        return [
            pltpu.make_async_copy(src, dst, link_sem.at[i])
            for i, (src, dst) in enumerate(((near_in, near), (far_in, far)))
        ]

    lane = lax.broadcasted_iota(jnp.int32, (rank, 2 * rank), 1)
    left = lane < rank
    side = jnp.where(left, 0, 1)

    def build(level):
        tr_copy(level).wait()

        def one(n, carry):
            rows = pl.ds(pl.multiple_of(n * rank, rank), rank)
            for links, count, first in ((near, nodes, 0), (far, SEND, nodes)):
                pair = tv[level, n, :, pl.ds(0 if first == 0 else 2 * rank, 2 * rank)].astype(jnp.float32)
                turned = pltpu.roll(pair, rank, 1)
                one_link = links[0, n, level]
                two_link = links[1, n, level]
                at_pair = jnp.where(left, one_link, two_link) - side
                at_turned = jnp.where(left, two_link, one_link) - side
                for j in range(count // 2):
                    spread = jnp.where(at_pair == 2 * j, pair, 0.0) + jnp.where(at_turned == 2 * j, turned, 0.0)
                    w[level, rows, pl.ds((first + 2 * j) * rank, 2 * rank)] = spread.astype(w.dtype)
            return carry

        lax.fori_loop(0, nodes, one, 0)

    def product(level, s, first):
        stacked = z[level, s].reshape((nodes + SEND) * rank, cols)
        summed = jnp.dot(w[level, pl.ds(first * rank, lead), :], stacked, preferred_element_type=jnp.float32)
        z[out_place(level), s, pl.ds(first, SEND)] = summed.astype(z.dtype).reshape(SEND, rank, cols)

    def step(level, s, then):
        if level == 0:
            leaf_copy(s).wait()
        exchange(level, s).wait_recv()
        product(level, s, 0)
        if then is not None:
            then()
        product(level, s, SEND)
        if level + 1 == half:
            z[half, s, q] = z[pre, s, q]
        if level + 1 == levels:
            out_copy(s).start()

    for copy in link_copies():
        copy.start()
    barrier = pltpu.get_barrier_semaphore()
    for bit in range(box_bits):
        pl.semaphore_signal(barrier, inc=1, device_id=partner(bit), device_id_type=MESH)
    for r in range(1, groups):
        pl.semaphore_signal(barrier, inc=1, device_id=(lax.rem(q + r, groups), b), device_id_type=MESH)
    for s in range(CHUNKS):
        leaf_copy(s).start()
        if s == 0:
            tr_copy(0).start()
    for level in range(1, levels):
        tr_copy(level).start()
    pl.semaphore_wait(barrier, box_bits + groups - 1)
    for copy in link_copies():
        copy.wait()

    def level_of(i):
        return i if i < half else i - 1

    def begin(i, s):
        if i == half:
            for r in range(1, groups):
                switch(s, r).start()
        else:
            exchange(level_of(i), s).start()

    order = [int(digit) for digit in f"{ORDER:x}"[1:]]
    at = [0] * CHUNKS
    built = 0
    while order:
        s = order.pop(0)
        if s == BUILD:
            build(built)
            built += 1
            continue
        i, working = divmod(at[s], 2)
        at[s] += 1
        if not working:
            begin(i, s)
        elif i == half:
            for r in range(1, groups):
                switch(s, r).wait_recv()
        else:
            early = i + 1 != half and order[:1] == [s]
            if early:
                order.pop(0)
                at[s] += 1
            step(level_of(i), s, functools.partial(begin, i + 1, s) if early else None)

    for s in range(CHUNKS):
        for level in range(levels):
            exchange(level, s).wait_send()
        for r in range(1, groups):
            switch(s, r).wait_send()
        out_copy(s).wait()


def on_device(leaves, translate, local_links, remote_links):
    nodes, rank, traces = leaves.shape
    levels = translate.shape[0]
    groups = lax.axis_size("grp")
    box_bits = lax.axis_size("box").bit_length() - 1
    cols = traces // CHUNKS
    width = nodes + SEND
    sizes = (levels, nodes, rank, cols, groups, box_bits)
    anywhere = pl.BlockSpec(memory_space=pl.ANY)
    dma = pltpu.SemaphoreType.DMA
    return pl.pallas_call(
        functools.partial(kernel, sizes),
        out_shape=jax.ShapeDtypeStruct(leaves.shape, leaves.dtype),
        in_specs=[anywhere] * 4,
        out_specs=anywhere,
        scratch_shapes=[
            pltpu.VMEM((levels + 2, CHUNKS, width, rank, cols), leaves.dtype),
            pltpu.VMEM((levels, nodes * rank, width * rank), leaves.dtype),
            pltpu.VMEM(translate.shape, translate.dtype),
            pltpu.SMEM((2, nodes, levels), local_links.dtype),
            pltpu.SMEM((2, nodes, levels), remote_links.dtype),
            dma((2,)),
            dma((levels, CHUNKS)),
            dma((levels, CHUNKS)),
            dma((CHUNKS, groups - 1)),
            dma((CHUNKS, groups - 1)),
            dma((CHUNKS,)),
            dma((levels,)),
            dma((CHUNKS,)),
        ],
        name="butterfly",
        compiler_params=pltpu.CompilerParams(
            collective_id=0, has_side_effects=True, vmem_limit_bytes=49 << 20
        ),
    )(leaves, translate, local_links.transpose(1, 2, 0), remote_links.transpose(1, 2, 0))


def solution(mesh):
    placed = (
        P(("grp", "box"), None, None),
        P(None, ("grp", "box"), None, None),
        P(None, None, ("grp", "box")),
        P(None, None, ("grp", "box")),
    )
    return jax.shard_map(
        on_device,
        mesh=mesh,
        in_specs=placed,
        out_specs=P(("grp", "box"), None, None),
        check_vma=False,
    )
```

```python
import functools

import jax
import jax.numpy as jnp
from jax import lax
from jax.experimental import pallas as pl
from jax.experimental.pallas import tpu as pltpu
from jax.sharding import PartitionSpec as P

MESH = pl.DeviceIdType.MESH
SEND = 4
CHUNKS = 8
BUILD = 8
READ_AHEAD = 2
ORDER = 0xf4808544008744185500744170365205844757513828320014477152354460012170640742325815464177360350257271140564063851717304045587712686251307307421243371576630032621515673327661331025656223314461576722303662581127036631225466326


def flipped(index, mask):
    return index + mask - 2 * mask * lax.rem(index // mask, 2)


def kernel(
    sizes, leaves, translate, near_in, far_in, out, z, w, tv, near, far, link_sem, send, recv, sw_send, sw_recv, leaf_sem, tr_sem, out_sem
):
    levels, nodes, rank, cols, groups, box_bits = sizes
    half = levels // 2
    pre, last = levels, levels + 1
    q = lax.axis_index("grp")
    b = lax.axis_index("box")
    lead = SEND * rank
    depth = nodes * rank

    def partner(level):
        return (q, flipped(b, 1 << (level % half % box_bits)))

    def columns(s):
        return pl.ds(s * cols, cols)

    def out_place(level):
        return pre if level == half - 1 else last if level == levels - 1 else level + 1

    def exchange(level, s):
        if level == 0:
            src = leaves.at[pl.ds(0, SEND), :, columns(s)]
        else:
            src = z.at[level, s, pl.ds(0, SEND)]
        return pltpu.make_async_remote_copy(
            src,
            z.at[level, s, pl.ds(nodes, SEND)],
            send.at[level, s],
            recv.at[level, s],
            device_id=partner(level),
            device_id_type=MESH,
        )

    def switch(s, r):
        to = lax.rem(q + r, groups)
        return pltpu.make_async_remote_copy(
            z.at[pre, s, to],
            z.at[half, s, q],
            sw_send.at[s, r - 1],
            sw_recv.at[s, r - 1],
            device_id=(to, b),
            device_id_type=MESH,
        )

    def leaf_copy(s):
        return pltpu.make_async_copy(
            leaves.at[:, :, columns(s)], z.at[0, s, pl.ds(0, nodes)], leaf_sem.at[s]
        )

    def tr_copy(level):
        return pltpu.make_async_copy(translate.at[level], tv.at[level], tr_sem.at[level])

    def out_copy(s):
        return pltpu.make_async_copy(
            z.at[last, s, pl.ds(0, nodes)], out.at[:, :, columns(s)], out_sem.at[s]
        )

    def link_copies():
        return [
            pltpu.make_async_copy(src, dst, link_sem.at[i])
            for i, (src, dst) in enumerate(((near_in, near), (far_in, far)))
        ]

    lane = lax.broadcasted_iota(jnp.int32, (rank, 2 * rank), 1)
    left = lane < rank
    side = jnp.where(left, 0, 1)

    def build(level):
        if level == 0:
            for copy in link_copies():
                copy.wait()
        tr_copy(level).wait()
        if level + READ_AHEAD < levels:
            tr_copy(level + READ_AHEAD).start()

        def one(n, carry):
            rows = pl.ds(pl.multiple_of(n * rank, rank), rank)
            for links, count, first in ((near, nodes, 0), (far, SEND, nodes)):
                pair = tv[level, n, :, pl.ds(0 if first == 0 else 2 * rank, 2 * rank)].astype(jnp.float32)
                turned = pltpu.roll(pair, rank, 1)
                one_link = links[0, n, level]
                two_link = links[1, n, level]
                at_pair = jnp.where(left, one_link, two_link) - side
                at_turned = jnp.where(left, two_link, one_link) - side
                for j in range(count // 2):
                    spread = jnp.where(at_pair == 2 * j, pair, 0.0) + jnp.where(at_turned == 2 * j, turned, 0.0)
                    w[level, rows, pl.ds((first + 2 * j) * rank, 2 * rank)] = spread.astype(w.dtype)
            return carry

        lax.fori_loop(0, nodes, one, 0)

    def product(level, s, first):
        stacked = z[level, s].reshape((nodes + SEND) * rank, cols)
        summed = jnp.dot(w[level, pl.ds(first * rank, lead), :], stacked, preferred_element_type=jnp.float32)
        z[out_place(level), s, pl.ds(first, SEND)] = summed.astype(z.dtype).reshape(SEND, rank, cols)

    def step(level, s, then):
        if level == 0:
            leaf_copy(s).wait()
        exchange(level, s).wait_recv()
        product(level, s, 0)
        if then is not None:
            then()
        product(level, s, SEND)
        if level + 1 == half:
            z[half, s, q] = z[pre, s, q]
        if level + 1 == levels:
            out_copy(s).start()

    barrier = pltpu.get_barrier_semaphore()
    for bit in range(box_bits):
        pl.semaphore_signal(barrier, inc=1, device_id=partner(bit), device_id_type=MESH)
    for r in range(1, groups):
        pl.semaphore_signal(barrier, inc=1, device_id=(lax.rem(q + r, groups), b), device_id_type=MESH)
    for copy in link_copies():
        copy.start()
    for level in range(READ_AHEAD):
        tr_copy(level).start()
    pl.semaphore_wait(barrier, box_bits + groups - 1)

    def level_of(i):
        return i if i < half else i - 1

    def begin(i, s):
        if i == half:
            for r in range(1, groups):
                switch(s, r).start()
        else:
            exchange(level_of(i), s).start()
        if i == 0:
            leaf_copy(s).start()

    order = [int(digit) for digit in f"{ORDER:x}"[1:]]
    at = [0] * CHUNKS
    built = 0
    while order:
        s = order.pop(0)
        if s == BUILD:
            build(built)
            built += 1
            continue
        i, working = divmod(at[s], 2)
        at[s] += 1
        if not working:
            begin(i, s)
        elif i == half:
            for r in range(1, groups):
                switch(s, r).wait_recv()
        else:
            early = i + 1 != half and order[:1] == [s]
            if early:
                order.pop(0)
                at[s] += 1
            step(level_of(i), s, functools.partial(begin, i + 1, s) if early else None)

    for s in range(CHUNKS):
        for level in range(levels):
            exchange(level, s).wait_send()
        for r in range(1, groups):
            switch(s, r).wait_send()
        out_copy(s).wait()


def on_device(leaves, translate, local_links, remote_links):
    nodes, rank, traces = leaves.shape
    levels = translate.shape[0]
    groups = lax.axis_size("grp")
    box_bits = lax.axis_size("box").bit_length() - 1
    cols = traces // CHUNKS
    width = nodes + SEND
    sizes = (levels, nodes, rank, cols, groups, box_bits)
    anywhere = pl.BlockSpec(memory_space=pl.ANY)
    dma = pltpu.SemaphoreType.DMA
    return pl.pallas_call(
        functools.partial(kernel, sizes),
        out_shape=jax.ShapeDtypeStruct(leaves.shape, leaves.dtype),
        in_specs=[anywhere] * 4,
        out_specs=anywhere,
        scratch_shapes=[
            pltpu.VMEM((levels + 2, CHUNKS, width, rank, cols), leaves.dtype),
            pltpu.VMEM((levels, nodes * rank, width * rank), leaves.dtype),
            pltpu.VMEM(translate.shape, translate.dtype),
            pltpu.SMEM((2, nodes, levels), local_links.dtype),
            pltpu.SMEM((2, nodes, levels), remote_links.dtype),
            dma((2,)),
            dma((levels, CHUNKS)),
            dma((levels, CHUNKS)),
            dma((CHUNKS, groups - 1)),
            dma((CHUNKS, groups - 1)),
            dma((CHUNKS,)),
            dma((levels,)),
            dma((CHUNKS,)),
        ],
        name="butterfly",
        compiler_params=pltpu.CompilerParams(
            collective_id=0, has_side_effects=True, vmem_limit_bytes=60 << 20
        ),
    )(leaves, translate, local_links.transpose(1, 2, 0), remote_links.transpose(1, 2, 0))


def solution(mesh):
    placed = (
        P(("grp", "box"), None, None),
        P(None, ("grp", "box"), None, None),
        P(None, None, ("grp", "box")),
        P(None, None, ("grp", "box")),
    )
    return jax.shard_map(
        on_device,
        mesh=mesh,
        in_specs=placed,
        out_specs=P(("grp", "box"), None, None),
        check_vma=False,
    )
```

```python
import functools

import jax
import jax.numpy as jnp
from jax import lax
from jax.experimental import pallas as pl
from jax.experimental.pallas import tpu as pltpu
from jax.sharding import PartitionSpec as P

MESH = pl.DeviceIdType.MESH
SEND = 4
CHUNKS = 8
BUILD = 8
READ_AHEAD = 2
ORDER = 0xf4808544008744185500744170365205844757513828320014477152354460012170640742325815464177360350257271140564063851717304045587712686251307307421243371576630032621515673327661331025656223314461576722303662581127036631225466326


def flipped(index, mask):
    return index + mask - 2 * mask * lax.rem(index // mask, 2)


def kernel(
    sizes, leaves, translate, links_in, out, z, w, tv, links, link_sem, send, recv, sw_send, sw_recv, leaf_sem, tr_sem
):
    levels, nodes, rank, cols, groups, box_bits = sizes
    half = levels // 2
    pre = levels
    q = lax.axis_index("grp")
    b = lax.axis_index("box")
    lead = SEND * rank
    depth = nodes * rank

    def partner(level):
        return (q, flipped(b, 1 << (level % half % box_bits)))

    def columns(s):
        return pl.ds(s * cols, cols)

    def out_place(level):
        return pre if level == half - 1 else level + 1

    def exchange(level, s):
        if level == 0:
            src = leaves.at[pl.ds(0, SEND), :, columns(s)]
        else:
            src = z.at[level, s, pl.ds(0, SEND)]
        return pltpu.make_async_remote_copy(
            src,
            z.at[level, s, pl.ds(nodes, SEND)],
            send.at[level, s],
            recv.at[level, s],
            device_id=partner(level),
            device_id_type=MESH,
        )

    def switch(s, r):
        to = lax.rem(q + r, groups)
        return pltpu.make_async_remote_copy(
            z.at[pre, s, to],
            z.at[half, s, q],
            sw_send.at[s, r - 1],
            sw_recv.at[s, r - 1],
            device_id=(to, b),
            device_id_type=MESH,
        )

    def leaf_copy(s):
        return pltpu.make_async_copy(
            leaves.at[:, :, columns(s)], z.at[0, s, pl.ds(0, nodes)], leaf_sem.at[s]
        )

    def tr_copy(level):
        return pltpu.make_async_copy(translate.at[level], tv.at[level], tr_sem.at[level])

    link_copy = pltpu.make_async_copy(links_in, links, link_sem)

    lane = lax.broadcasted_iota(jnp.int32, (rank, 2 * rank), 1)
    left = lane < rank
    side = jnp.where(left, 0, 1)

    def build(level):
        if level == 0:
            link_copy.wait()
        tr_copy(level).wait()
        if level + READ_AHEAD < levels:
            tr_copy(level + READ_AHEAD).start()

        def one(n, carry):
            rows = pl.ds(pl.multiple_of(n * rank, rank), rank)
            for kind, count, first in ((0, nodes, 0), (1, SEND, nodes)):
                pair = tv[level, n, :, pl.ds(0 if first == 0 else 2 * rank, 2 * rank)].astype(jnp.float32)
                turned = pltpu.roll(pair, rank, 1)
                one_link = links[kind, 0, n, level]
                two_link = links[kind, 1, n, level]
                at_pair = jnp.where(left, one_link, two_link) - side
                at_turned = jnp.where(left, two_link, one_link) - side
                for j in range(count // 2):
                    spread = jnp.where(at_pair == 2 * j, pair, 0.0) + jnp.where(at_turned == 2 * j, turned, 0.0)
                    w[level, rows, pl.ds((first + 2 * j) * rank, 2 * rank)] = spread.astype(w.dtype)
            return carry

        lax.fori_loop(0, nodes, one, 0)

    def product(level, s, first):
        stacked = z[level, s].reshape((nodes + SEND) * rank, cols)
        summed = jnp.dot(w[level, pl.ds(first * rank, lead), :], stacked, preferred_element_type=jnp.float32)
        made = summed.astype(z.dtype).reshape(SEND, rank, cols)
        if level + 1 == levels:
            out[pl.ds(first, SEND), :, columns(s)] = made
        else:
            z[out_place(level), s, pl.ds(first, SEND)] = made

    def step(level, s, then):
        if level == 0:
            leaf_copy(s).wait()
        exchange(level, s).wait_recv()
        product(level, s, 0)
        if then is not None:
            then()
        product(level, s, SEND)
        if level + 1 == half:
            z[half, s, q] = z[pre, s, q]

    barrier = pltpu.get_barrier_semaphore()
    for bit in range(box_bits):
        pl.semaphore_signal(barrier, inc=1, device_id=partner(bit), device_id_type=MESH)
    for r in range(1, groups):
        pl.semaphore_signal(barrier, inc=1, device_id=(lax.rem(q + r, groups), b), device_id_type=MESH)
    link_copy.start()
    for level in range(READ_AHEAD):
        tr_copy(level).start()
    pl.semaphore_wait(barrier, box_bits + groups - 1)

    def level_of(i):
        return i if i < half else i - 1

    def begin(i, s):
        if i == half:
            for r in range(1, groups):
                switch(s, r).start()
        else:
            exchange(level_of(i), s).start()
        if i == 0:
            leaf_copy(s).start()

    order = [int(digit) for digit in f"{ORDER:x}"[1:]]
    at = [0] * CHUNKS
    built = 0
    while order:
        s = order.pop(0)
        if s == BUILD:
            build(built)
            built += 1
            continue
        i, working = divmod(at[s], 2)
        at[s] += 1
        if not working:
            begin(i, s)
        elif i == half:
            for r in range(1, groups):
                switch(s, r).wait_recv()
        else:
            early = i + 1 != half and order[:1] == [s]
            if early:
                order.pop(0)
                at[s] += 1
            step(level_of(i), s, functools.partial(begin, i + 1, s) if early else None)

    for s in range(CHUNKS):
        for level in range(levels):
            exchange(level, s).wait_send()
        for r in range(1, groups):
            switch(s, r).wait_send()


def on_device(leaves, translate, local_links, remote_links):
    nodes, rank, traces = leaves.shape
    levels = translate.shape[0]
    groups = lax.axis_size("grp")
    box_bits = lax.axis_size("box").bit_length() - 1
    cols = traces // CHUNKS
    width = nodes + SEND
    sizes = (levels, nodes, rank, cols, groups, box_bits)
    anywhere = pl.BlockSpec(memory_space=pl.ANY)
    dma = pltpu.SemaphoreType.DMA
    return pl.pallas_call(
        functools.partial(kernel, sizes),
        out_shape=jax.ShapeDtypeStruct(leaves.shape, leaves.dtype),
        in_specs=[anywhere] * 3,
        out_specs=pl.BlockSpec(memory_space=pltpu.VMEM),
        scratch_shapes=[
            pltpu.VMEM((levels + 1, CHUNKS, width, rank, cols), leaves.dtype),
            pltpu.VMEM((levels, nodes * rank, width * rank), leaves.dtype),
            pltpu.VMEM(translate.shape, translate.dtype),
            pltpu.SMEM((2, 2, nodes, levels), local_links.dtype),
            dma,
            dma((levels, CHUNKS)),
            dma((levels, CHUNKS)),
            dma((CHUNKS, groups - 1)),
            dma((CHUNKS, groups - 1)),
            dma((CHUNKS,)),
            dma((levels,)),
        ],
        name="butterfly",
        compiler_params=pltpu.CompilerParams(
            collective_id=0, has_side_effects=True, vmem_limit_bytes=52 << 20
        ),
    )(leaves, translate, jnp.stack([local_links, remote_links]).transpose(0, 2, 3, 1))


def solution(mesh):
    placed = (
        P(("grp", "box"), None, None),
        P(None, ("grp", "box"), None, None),
        P(None, None, ("grp", "box")),
        P(None, None, ("grp", "box")),
    )
    return jax.shard_map(
        on_device,
        mesh=mesh,
        in_specs=placed,
        out_specs=P(("grp", "box"), None, None),
        check_vma=False,
    )
```
